32 devices in a mesh: row: 4 (over y, x), col: 8 (over z, core).
Axes of the slice: x: 2, y: 2, z: 4, core: 2. Of those that a mesh axis runs over, the one named last changes fastest.
Arguments:
- tiles: bfloat16 [3072, 128, 128], P(('row', 'col')), may hold values from -0.5 to 0.5
- tile_rows: int32 [3072], P(('row', 'col')), may hold values from 0 to 15
- tile_cols: int32 [3072], P(('row', 'col')), may hold values from 0 to 7
- counts: int32 [32], P(('row', 'col')), may hold values from 32 to 96, as said below
- omega: bfloat16 [8192, 256], P('col'), may hold values from -6 to 6
Outputs:
- basis: bfloat16 [8192, 256], P(('row', 'col'))
- projected: bfloat16 [8192, 256], P('col')
The draws below stay inside these ranges and needn't reach their ends.
Inputs may be any that keep to these rules, and one draw needn't show every extreme that they name: `counts`: within one device the live and dead slots name distinct blocks; some device has all 96 slots live and some has 32.
All inputs are finite; a program needn't handle non-finite values.
Results may differ from the reference program's by a relative error of at most 0.0095.
Values may be sent and summed in bfloat16 or wider, within the bound.
No kernel may reach another device: no remote copies, remote signals or barrier semaphores. Data moves between devices by JAX's collectives and lax.ppermute only.
A program may use at most 128 MiB of HBM per device.

```python
import jax
import jax.numpy as jnp
from jax import lax

B = 128
K = 256
RB_DEV = 16
CB_DEV = 8
SLOTS = 96
NR = 8192
NC = 8192
TILES = 3072
N_ROW = 4
N_COL = 8


def block_positions(key):
    keys = jax.random.split(key, N_ROW * N_COL)
    perms = jax.vmap(lambda k: jax.random.permutation(k, RB_DEV * CB_DEV))(keys)
    return perms[:, :SLOTS].reshape(-1).astype(jnp.int32)


def draw_tile_rows(key, part):
    places = block_positions(key)
    return (places // CB_DEV).astype(jnp.int32)


def draw_tile_cols(key, part):
    places = block_positions(key)
    return (places % CB_DEV).astype(jnp.int32)


def draw_counts(key, part):
    key = jax.random.fold_in(key, 7)
    devices = N_ROW * N_COL
    values = jax.random.randint(key, (devices,), SLOTS // 3, SLOTS + 1).astype(jnp.int32)
    order = jax.random.permutation(jax.random.fold_in(key, 1), devices)
    values = values.at[order[0]].set(SLOTS)
    values = values.at[order[1]].set(SLOTS // 3)
    return values.astype(jnp.int32)


def block_scale(key, shape, cuts, least, top_value):
    gain = 1.0
    for position, parts in cuts:
        steps = jax.random.uniform(jax.random.fold_in(jax.random.fold_in(key, 6), position), (parts,), jnp.float32, least / len(cuts), top_value / len(cuts))
        gain = gain * jnp.repeat(jnp.exp(steps), shape[position] // parts).reshape((-1,) + (1,) * (len(shape) - 1 - position))
    return gain


def scatter_about(stream_key, shape, width, bound, pieces=(), kind=jnp.bfloat16):
    entries = jax.random.normal(stream_key, shape, jnp.float32) * width
    if len(pieces) > 0:
        entries = block_scale(stream_key, shape, pieces, -0.22, 0.18) * entries
    return jnp.clip(entries, min=-bound, max=bound).astype(kind)


def setup_inputs(seed: int = 0) -> dict:
    arg_keys = jax.random.split(jax.random.key(seed), 6)
    tiles = scatter_about(arg_keys[0], (TILES, B, B), B ** -0.5, 0.5, ((0, 32),))
    tile_rows = draw_tile_rows(jax.random.fold_in(arg_keys[5], 71), 0)
    tile_cols = draw_tile_cols(jax.random.fold_in(arg_keys[5], 71), 0)
    counts = draw_counts(jax.random.fold_in(arg_keys[5], 71), 0)
    omega = scatter_about(arg_keys[4], (NC, K), 1.0, 6.0, ((0, 8),))
    return {"tiles": tiles, "tile_rows": tile_rows, "tile_cols": tile_cols, "counts": counts, "omega": omega}


def reference(tiles, tile_rows, tile_cols, counts, omega):
    devices = N_ROW * N_COL
    tile_set = tiles.reshape(devices, SLOTS, B, B)
    row_set = tile_rows.reshape(devices, SLOTS)
    col_set = tile_cols.reshape(devices, SLOTS)
    omega_blocks = omega.reshape(CB_DEV * N_COL, B, K)
    slot_ids = jnp.arange(SLOTS, dtype=jnp.int32)

    def live_of(index):
        return (slot_ids < counts[index]).astype(jnp.float32)

    def sketch_step(carry, index):
        grow = index // N_COL * RB_DEV + row_set[index]
        gcol = index % N_COL * CB_DEV + col_set[index]
        picked = omega_blocks[gcol].astype(jnp.float32)
        terms = jnp.einsum('sij,sjk->sik', tile_set[index].astype(jnp.float32), picked)
        terms = terms * live_of(index)[:, None, None]
        return (carry.at[grow].add(terms), None)
    index_list = jnp.arange(devices, dtype=jnp.int32)
    sketch0 = jnp.zeros((RB_DEV * N_ROW, B, K), jnp.float32)
    sketch, _ = lax.scan(sketch_step, sketch0, index_list)
    sketch = sketch.reshape(NR, K)
    gram = jnp.dot(sketch.T, sketch, precision=lax.Precision.HIGHEST)
    lower = jnp.linalg.cholesky(gram)
    solved = jax.scipy.linalg.solve_triangular(lower, sketch.T, lower=True).T
    basis = (solved * jnp.sqrt(jnp.float32(NR))).astype(jnp.bfloat16)
    basis_blocks = basis.reshape(RB_DEV * N_ROW, B, K)

    def project_step(carry, index):
        grow = index // N_COL * RB_DEV + row_set[index]
        gcol = index % N_COL * CB_DEV + col_set[index]
        picked = basis_blocks[grow].astype(jnp.float32)
        terms = jnp.einsum('sji,sjk->sik', tile_set[index].astype(jnp.float32), picked)
        terms = terms * live_of(index)[:, None, None]
        return (carry.at[gcol].add(terms), None)
    proj0 = jnp.zeros((CB_DEV * N_COL, B, K), jnp.float32)
    projected, _ = lax.scan(project_step, proj0, index_list)
    projected = projected.reshape(NC, K) / jnp.sqrt(jnp.float32(RB_DEV * N_ROW))
    return (basis, projected.astype(jnp.bfloat16))
```

```python
import functools

import jax
import jax.numpy as jnp
from jax import lax
from jax.experimental import pallas as pl
from jax.experimental.pallas import tpu as pltpu
from jax.sharding import PartitionSpec as P

RB_DEV = 16
CORES = 2
MIB = 1024 * 1024
BF = jnp.bfloat16
F32 = jnp.float32

NT = (((1,), (1,)), ((), ()))
TN = (((0,), (0,)), ((), ()))


def vmem():
    return pl.BlockSpec(memory_space=pltpu.VMEM)


def smem():
    return pl.BlockSpec(memory_space=pltpu.SMEM)


def call(body, ins, outs, scratch=(), limit=24, flops=0, nbytes=0, name=None):
    return pl.pallas_call(
        body,
        out_shape=outs,
        in_specs=[smem() if scalar else vmem() for _, scalar in ins],
        out_specs=[vmem() for _ in outs],
        scratch_shapes=list(scratch),
        compiler_params=pltpu.CompilerParams(vmem_limit_bytes=limit * MIB),
        cost_estimate=pl.CostEstimate(flops=flops, bytes_accessed=nbytes, transcendentals=0),
        name=name,
    )(*[array for array, _ in ins])


def dot(a, b, dims=None):
    if dims is None:
        dims = (((1,), (0,)), ((), ()))
    return lax.dot_general(a, b, dims, preferred_element_type=F32)


def split(x):
    high = x.astype(BF)
    return high, (x - high.astype(F32)).astype(BF)


def dot3(a, b, dims=None):
    a_high, a_low = split(a)
    b_high, b_low = split(b)
    return dot(a_high, b_high, dims) + (dot(a_high, b_low, dims) + dot(a_low, b_high, dims))


def sketch_kernel(share, pos, counts, rows, cols, tiles, omega, sent, kept, dense):
    size_b = tiles.shape[1]
    dense[...] = jnp.zeros_like(dense)

    def place(slot, carry):
        start = pl.multiple_of(rows[slot] * size_b, size_b)
        dense[cols[slot], pl.ds(start, size_b), :] = tiles[slot]
        return carry

    lax.fori_loop(0, counts[0], place, 0)
    core = pos[1]
    for out, owner in ((sent, 1 - core), (kept, core)):
        for step in range(out.shape[0] // share):
            start = pl.multiple_of((step * CORES + owner) * share, share)
            left = jnp.concatenate([dense[c, pl.ds(start, share), :] for c in range(dense.shape[0])], axis=1)
            out[step * share : (step + 1) * share, :] = dot(left, omega[...]).astype(out.dtype)


def transpose_kernel(counts, rows, cols, tiles, turned):
    size_b = tiles.shape[1]
    turned[...] = jnp.zeros_like(turned)

    def place(slot, carry):
        start = pl.multiple_of(cols[slot] * size_b, size_b)
        turned[rows[slot], pl.ds(start, size_b), :] = tiles[slot].T
        return carry

    lax.fori_loop(0, counts[0], place, 0)


def pair_kernel(share, pos, kept, came, own, *sends):
    z = pos[0]
    for step in range(len(sends) + 1):
        start = pl.multiple_of((z ^ step) * share, share)
        rows = pl.ds(start, share)
        total = kept[rows, :] + came[rows, :].astype(F32)
        if step == 0:
            own[...] = total
        else:
            sends[step - 1][...] = total.astype(BF)


def sum_kernel(count, own, *refs):
    total = own[...]
    for ref in refs[:count]:
        total = total + ref[...].astype(F32)
    for out in refs[count:]:
        out[...] = total.astype(out.dtype)


def gram_kernel(share, zs, pos, *refs):
    chunks, (full, gram) = refs[: 2 * zs], refs[2 * zs :]
    z, core = pos[0], pos[1]
    for step in range(zs):
        for side in range(CORES):
            place = (z ^ step) * CORES + (core ^ side)
            full[pl.ds(pl.multiple_of(place * share, share), share), :] = chunks[step * CORES + side][...]
    half = gram.shape[0]

    for side in range(CORES):

        @pl.when(core == side)
        def _():
            gram[...] = dot(full[:, side * half : (side + 1) * half], full[...], TN)


def back_kernel(pos, turned, full, own, *sends):
    me = pos[2]
    share = own.shape[0]
    for step in range(len(sends) + 1):
        start = pl.multiple_of((me ^ step) * share, share)
        left = jnp.concatenate([turned[r, pl.ds(start, share), :] for r in range(turned.shape[0])], axis=1)
        product = dot(left, full[...])
        if step == 0:
            own[...] = product
        else:
            sends[step - 1][...] = product.astype(BF)


def factor_kernel(scale, pos, mine, other, rows, high, low, basis, work, norm_ref, inverse, trail):
    core = pos[1]
    half, size = mine.shape
    work[pl.ds(pl.multiple_of(core * half, half), half), :] = mine[...]
    work[pl.ds(pl.multiple_of((1 - core) * half, half), half), :] = other[...]
    gram = work[...]
    row_id = lax.broadcasted_iota(jnp.int32, (size, size), 0)
    col_id = lax.broadcasted_iota(jnp.int32, (size, size), 1)
    eye = (row_id == col_id).astype(F32)
    diagonal = gram * eye
    scale_col = lax.rsqrt(jnp.sum(diagonal, axis=1, keepdims=True))
    scale_row = lax.rsqrt(jnp.sum(diagonal, axis=0, keepdims=True))
    excess = gram * scale_col * scale_row - eye
    below = (row_id > col_id).astype(F32)
    phi_mask = below + 0.5 * eye
    keep_mask = below + 2.0 * eye
    phi = excess * phi_mask
    near = -phi
    for step in range(3):
        mul = dot3 if step == 2 else (lambda a, b, dims=None: dot(a.astype(BF), b.astype(BF), dims))
        turn = excess + mul(near, excess)
        rest = near * keep_mask + turn + mul(near + turn, near, NT)
        phi = rest * phi_mask
        near = near - phi - mul(phi, near)
    worst = jnp.max(jnp.abs(phi))
    inverse[...] = (near + eye) * scale_row
    converged = worst < 1e-2

    @pl.when(jnp.logical_not(converged))
    def _():
        trail[...] = gram * scale_col * scale_row
        inverse[...] = eye

        def eliminate(k, carry):
            row = trail[pl.ds(k, 1), :]
            pivot = jnp.sum(jnp.where(col_id[:1] == k, row, 0.0), axis=1, keepdims=True)
            column = jnp.sum(jnp.where(col_id == k, trail[...], 0.0), axis=1, keepdims=True)
            factor = jnp.where(row_id[:, :1] > k, column / pivot, 0.0)
            source = inverse[pl.ds(k, 1), :]
            inverse[...] = inverse[...] - factor * source
            inverse[pl.ds(k, 1), :] = source * lax.rsqrt(pivot)
            trail[...] = trail[...] - factor * row
            return carry

        lax.fori_loop(0, size, eliminate, 0)
        inverse[...] = inverse[...] * scale_row

    scaled = inverse[...] * scale
    high_part, low_part = split(scaled)
    high[...] = high_part
    low[...] = low_part
    row_high, row_low = split(rows[...])
    basis[...] = (
        dot(row_high, high_part, NT) + (dot(row_high, low_part, NT) + dot(row_low, high_part, NT))
    ).astype(BF)


def project_kernel(scale, pos, high, low, *refs):
    chunks, out = refs[:-1], refs[-1]
    me = pos[2]
    share = chunks[0].shape[0]
    for step, chunk in enumerate(chunks):
        start = pl.multiple_of((me ^ step) * share, share)
        product = dot(chunk[...], high[...], NT) + dot(chunk[...], low[...], NT)
        out[pl.ds(start, share), :] = (product * scale).astype(BF)


def tree_sum(terms):
    while len(terms) > 1:
        terms = [terms[i] + terms[i + 1] for i in range(0, len(terms), 2)]
    return terms[0]


def shards(tiles, tile_rows, tile_cols, counts, omega):
    size_b = tiles.shape[1]
    rank = omega.shape[1]
    cols_here = omega.shape[0]
    col_blocks = cols_here // size_b
    row_groups = lax.axis_size("row")
    col_groups = lax.axis_size("col")
    zs = col_groups // CORES
    rows_here = RB_DEV * size_b
    share = rows_here // col_groups
    back_share = cols_here // row_groups
    total_rows = rows_here * row_groups
    half = rank // CORES
    index_col = lax.axis_index("col")
    pos = jnp.stack([index_col // CORES, index_col % CORES, lax.axis_index("row")]).astype(jnp.int32)

    def swap_core(x):
        return lax.ppermute(x, "col", [(i, i ^ 1) for i in range(col_groups)])

    def swap_z(x, step):
        return lax.ppermute(x, "col", [(i, i ^ (CORES * step)) for i in range(col_groups)])

    def swap_row(x, step):
        return lax.ppermute(x, "row", [(i, i ^ step) for i in range(row_groups)])

    def array(shape, kind):
        return jax.ShapeDtypeStruct(shape, kind)

    part = (share, rank)
    sent, kept = call(
        functools.partial(sketch_kernel, share),
        [(pos, 1), (counts, 1), (tile_rows, 1), (tile_cols, 1), (tiles, 0), (omega, 0)],
        [array((zs * share, rank), BF), array((zs * share, rank), F32)],
        [pltpu.VMEM((col_blocks, rows_here, size_b), BF)],
        flops=2 * rows_here * cols_here * rank,
        nbytes=6 * MIB,
        name="sketch",
    )
    came = swap_core(sent)
    (turned,) = call(
        transpose_kernel,
        [(counts, 1), (tile_rows, 1), (tile_cols, 1), (tiles, 0)],
        [array((RB_DEV, cols_here, size_b), BF)],
        nbytes=8 * MIB,
        name="turn",
    )
    own, *sends = call(
        functools.partial(pair_kernel, share),
        [(pos, 1), (kept, 0), (came, 0)],
        [array(part, F32)] + [array(part, BF)] * (zs - 1),
        nbytes=2 * MIB,
        name="pair",
    )
    gets = [swap_z(x, k + 1) for k, x in enumerate(sends)]
    own_rows, own_short = call(
        functools.partial(sum_kernel, len(gets)),
        [(own, 0)] + [(x, 0) for x in gets],
        [array(part, F32), array(part, BF)],
        nbytes=MIB,
        name="rows",
    )
    chunks = []
    for k in range(zs):
        chunk = swap_z(own_short, k) if k else own_short
        chunks += [chunk, swap_core(chunk)]
    full, gram = call(
        functools.partial(gram_kernel, share, zs),
        [(pos, 1)] + [(x, 0) for x in chunks],
        [array((rows_here, rank), BF), array((half, rank), F32)],
        flops=2 * rows_here * rank * half,
        nbytes=2 * MIB,
        name="gram",
    )
    gram_half = tree_sum([gram] + [swap_row(gram, k) for k in range(1, row_groups)])
    gram_other = swap_core(gram_half)
    back_own, *back_sends = call(
        back_kernel,
        [(pos, 1), (turned, 0), (full, 0)],
        [array((back_share, rank), F32)] + [array((back_share, rank), BF)] * (row_groups - 1),
        flops=2 * rows_here * cols_here * rank,
        nbytes=6 * MIB,
        name="back",
    )
    back_gets = [swap_row(x, k + 1) for k, x in enumerate(back_sends)]
    (back_sum,) = call(
        functools.partial(sum_kernel, len(back_gets)),
        [(back_own, 0)] + [(x, 0) for x in back_gets],
        [array((back_share, rank), BF)],
        nbytes=MIB,
        name="columns",
    )
    back_all = [back_sum] + [swap_row(back_sum, k) for k in range(1, row_groups)]
    high, low, basis = call(
        functools.partial(factor_kernel, float(total_rows) ** 0.5),
        [(pos, 1), (gram_half, 0), (gram_other, 0), (own_rows, 0)],
        [array((rank, rank), BF), array((rank, rank), BF), array(part, BF)],
        [pltpu.VMEM((rank, rank), F32), pltpu.SMEM((1,), F32), pltpu.VMEM((rank, rank), F32), pltpu.VMEM((rank, rank), F32)],
        flops=2 * 20 * rank**3,
        nbytes=MIB,
        name="factor",
    )
    (projected,) = call(
        functools.partial(project_kernel, float(RB_DEV * row_groups) ** -0.5),
        [(pos, 1), (high, 0), (low, 0)] + [(x, 0) for x in back_all],
        [array((cols_here, rank), BF)],
        flops=4 * cols_here * rank * rank,
        nbytes=2 * MIB,
        name="project",
    )
    return basis, projected


def solution(mesh):
    return jax.shard_map(
        shards,
        mesh=mesh,
        in_specs=(
            P(("row", "col"), None, None),
            P(("row", "col")),
            P(("row", "col")),
            P(("row", "col")),
            P("col", None),
        ),
        out_specs=(P(("row", "col"), None), P("col", None)),
        check_vma=False,
    )
```

```python
import functools

import jax
import jax.numpy as jnp
from jax import lax
from jax.experimental import pallas as pl
from jax.experimental.pallas import tpu as pltpu
from jax.sharding import PartitionSpec as P

RB_DEV = 16
CORES = 2
LOADS = 4
TOKEN = (8, 128)
CODE = 256
LANES = 128
SKETCH_LIMIT = 50
TURN_LIMIT = 44
MIB = 1024 * 1024
BF = jnp.bfloat16
F32 = jnp.float32

NN = (((1,), (0,)), ((), ()))
NT = (((1,), (1,)), ((), ()))
TN = (((0,), (0,)), ((), ()))

SPACES = {"v": pltpu.VMEM, "s": pltpu.SMEM, "h": pltpu.HBM, "a": pl.ANY}


def call(name, body, ins, outs, scratch=(), limit=24, flops=0, nbytes=0):
    return pl.pallas_call(
        body,
        out_shape=outs,
        in_specs=[pl.BlockSpec(memory_space=SPACES[space]) for space, _ in ins],
        out_specs=[pl.BlockSpec(memory_space=pltpu.VMEM) for _ in outs],
        scratch_shapes=list(scratch),
        compiler_params=pltpu.CompilerParams(vmem_limit_bytes=limit * MIB),
        cost_estimate=pl.CostEstimate(flops=flops, bytes_accessed=nbytes, transcendentals=0),
        name=name,
    )(*[array for _, array in ins])


def dot(a, b, dims=NN):
    return lax.dot_general(a, b, dims, preferred_element_type=F32)


def dot_short(a, b, dims=NN):
    return dot(a.astype(BF), b.astype(BF), dims)


def split(x):
    high = x.astype(BF)
    return high, (x - high.astype(F32)).astype(BF)


def dot_long(a, b, dims=NN):
    a_high, a_low = split(a)
    b_high, b_low = split(b)
    return dot(a_high, b_high, dims) + (dot(a_high, b_low, dims) + dot(a_low, b_high, dims))


def place():
    col = lax.axis_index("col")
    return col // CORES, col % CORES


def far_first(count):
    return [count - 1] + list(range(1, count - 1))


def rows_at(index, count):
    return pl.ds(pl.multiple_of(index * count, count), count)


def put_live(codes, codes_smem, tiles_hbm, tiles, sems, clear, put):
    load = tiles.shape[0] // LOADS
    first = pltpu.make_async_copy(codes, codes_smem, sems.at[LOADS])
    first.start()
    copies = []
    for k in range(LOADS):
        piece = pl.ds(k * load, load)
        copies.append(pltpu.make_async_copy(tiles_hbm.at[piece], tiles.at[piece], sems.at[k]))
    for copy in copies:
        copy.start()
    clear()
    first.wait()

    def step(slot, carry):
        code = codes_smem[slot]
        put(slot, code // CODE, code % CODE)
        return carry

    live = codes_smem[tiles.shape[0]]
    for k, copy in enumerate(copies):
        copy.wait()
        lax.fori_loop(k * load, jnp.clip(live, k * load, (k + 1) * load), step, 0)


def sketch_kernel(share, codes, tiles_hbm, omega_hbm, sent, kept, codes_smem, tiles, omega, dense, sems):
    size_b = tiles.shape[1]
    last = pltpu.make_async_copy(omega_hbm, omega, sems.at[LOADS + 1])
    last.start()

    def clear():
        dense[...] = jnp.zeros_like(dense)

    def put(slot, row, col):
        dense[col, rows_at(row, size_b), :] = tiles[slot]

    put_live(codes, codes_smem, tiles_hbm, tiles, sems, clear, put)
    last.wait()
    _, core = place()
    for out, owner in ((sent, 1 - core), (kept, core)):
        for step in range(out.shape[0] // share):
            here = rows_at(step * CORES + owner, share)
            left = jnp.concatenate([dense[c, here, :] for c in range(dense.shape[0])], axis=1)
            out[step * share : (step + 1) * share, :] = dot(left, omega[...]).astype(out.dtype)


def turn_kernel(codes, tiles_hbm, _, turned, token, codes_smem, tiles, sems):
    size_b = tiles.shape[1]
    token[...] = jnp.zeros_like(token)

    def clear():
        turned[...] = jnp.zeros_like(turned)

    def put(slot, row, col):
        turned[row, rows_at(col, size_b), :] = tiles[slot].T

    put_live(codes, codes_smem, tiles_hbm, tiles, sems, clear, put)


def pair_kernel(share, kept, came, own, token, *sends):
    z, _ = place()
    token[...] = jnp.zeros_like(token)
    for step in range(len(sends) + 1):
        here = rows_at(z ^ step, share)
        total = kept[here, :] + came[here, :].astype(F32)
        if step == 0:
            own[...] = total
        else:
            sends[step - 1][...] = total.astype(BF)


def columns_kernel(count, own, *refs):
    total = own[...]
    for ref in refs[:count]:
        total = total + ref[...].astype(F32)
    refs[count][...] = total.astype(BF)


def tree_kernel(own, *refs):
    refs[-1][...] = tree_sum([own[...]] + [ref[...] for ref in reversed(refs[:-1])])


def tree_sum(terms):
    while len(terms) > 1:
        terms = [terms[i] + terms[i + 1] for i in range(0, len(terms), 2)]
    return terms[0]


def rows_kernel(count, own, *refs):
    total = own[...]
    for ref in refs[:count]:
        total = total + ref[...].astype(F32)
    refs[-2][...] = total
    refs[-1][...] = total.astype(BF)


def pack_kernel(order, own, *refs):
    out = refs[-1]
    z, _ = place()
    share = own.shape[0]
    out[rows_at(z, share), :] = own[...]
    for step, ref in zip(order, refs):
        out[rows_at(z ^ step, share), :] = ref[...]


def full_kernel(share, mine, other, full):
    _, core = place()
    for z in range(mine.shape[0] // share):
        here = slice(z * share, (z + 1) * share)
        full[rows_at(z * CORES + core, share), :] = mine[here, :]
        full[rows_at(z * CORES + (1 - core), share), :] = other[here, :]


def back_kernel(turned, full, own, gram, *sends):
    me = lax.axis_index("row")
    _, core = place()
    share = own.shape[0]
    half = gram.shape[1]
    quarter = half // CORES
    for side in range(CORES):

        @pl.when(core == side)
        def _():
            diagonal = full[:, side * half : (side + 1) * half]
            gram[:half, :] = dot(diagonal, diagonal, TN)
            lower = full[:, half + side * quarter : half + (side + 1) * quarter]
            gram[half:, :] = dot(lower, full[:, :half], TN)

    for step in list(range(1, len(sends) + 1)) + [0]:
        here = rows_at(me ^ step, share)
        left = jnp.concatenate([turned[r, here, :] for r in range(turned.shape[0])], axis=1)
        product = dot(left, full[...])
        if step == 0:
            own[...] = product
        else:
            sends[step - 1][...] = product.astype(BF)


def factor_kernel(scale, *refs):
    mine, other, rows, high, low, basis, work, inverse = refs
    _, core = place()
    size = work.shape[0]
    half, quarter = size // CORES, size // (2 * CORES)
    for source, owner in ((mine, core), (other, 1 - core)):
        for side in range(CORES):

            @pl.when(owner == side)
            def _():
                work[side * half : (side + 1) * half, side * half : (side + 1) * half] = source[:half, :]
                here = slice(half + side * quarter, half + (side + 1) * quarter)
                work[here, :half] = source[half:, :]
    work[:half, half:] = work[half:, :half].T
    gram = work[...]
    row_id = lax.broadcasted_iota(jnp.int32, (size, size), 0)
    col_id = lax.broadcasted_iota(jnp.int32, (size, size), 1)
    eye = (row_id == col_id).astype(F32)
    diagonal = gram * eye
    scale_col = lax.rsqrt(jnp.sum(diagonal, axis=1, keepdims=True))
    scale_row = lax.rsqrt(jnp.sum(diagonal, axis=0, keepdims=True))
    excess = gram * scale_col * scale_row - eye
    below = (row_id > col_id).astype(F32)
    phi_mask = below + 0.5 * eye
    keep_mask = below + 2.0 * eye
    near = -(excess * phi_mask)
    for step in range(3):
        mul = dot_long if step == 2 else dot_short
        turn = excess + mul(near, excess)
        rest = near * keep_mask + turn + mul(near + turn, near, NT)
        phi = rest * phi_mask
        near = near - phi - mul(phi, near)
    inverse[...] = (near + eye) * scale_row
    converged = jnp.max(jnp.abs(phi)) < 1e-2

    @pl.when(jnp.logical_not(converged))
    def _():
        work[...] = gram * scale_col * scale_row
        inverse[...] = eye

        def eliminate(k, carry):
            row = work[pl.ds(k, 1), :]
            pivot = jnp.sum(jnp.where(col_id[:1] == k, row, 0.0), axis=1, keepdims=True)
            column = jnp.sum(jnp.where(col_id == k, work[...], 0.0), axis=1, keepdims=True)
            factor = jnp.where(row_id[:, :1] > k, column / pivot, 0.0)
            source = inverse[pl.ds(k, 1), :]
            inverse[...] = inverse[...] - factor * source
            inverse[pl.ds(k, 1), :] = source * lax.rsqrt(pivot)
            work[...] = work[...] - factor * row
            return carry

        lax.fori_loop(0, size, eliminate, 0)
        inverse[...] = inverse[...] * scale_row

    high_part, low_part = split(inverse[...] * scale)
    high[...] = high_part
    low[...] = low_part
    row_high, row_low = split(rows[...])
    basis[...] = (
        dot(row_high, high_part, NT) + (dot(row_high, low_part, NT) + dot(row_low, high_part, NT))
    ).astype(BF)


def project_kernel(scale, count, high, low, *refs):
    out = refs[-1]
    me = lax.axis_index("row")
    share = refs[0].shape[0]
    for index, step in enumerate([0] + list(reversed(range(1, count)))):
        chunk = refs[index][...]
        product = dot(chunk, high[...], NT) + dot(chunk, low[...], NT)
        out[rows_at(me ^ step, share), :] = (product * scale).astype(BF)


def shards(tiles, tile_rows, tile_cols, counts, omega):
    slots, size_b, _ = tiles.shape
    rank = omega.shape[1]
    cols_here = omega.shape[0]
    col_blocks = cols_here // size_b
    row_groups = lax.axis_size("row")
    col_groups = lax.axis_size("col")
    zs = col_groups // CORES
    rows_here = RB_DEV * size_b
    share = rows_here // col_groups
    back_share = cols_here // row_groups
    total_rows = rows_here * row_groups

    def swap_core(x):
        return lax.ppermute(x, "col", [(i, i ^ 1) for i in range(col_groups)])

    def swap_z(x, step):
        return lax.ppermute(x, "col", [(i, i ^ (CORES * step)) for i in range(col_groups)])

    def swap_row(x, step):
        return lax.ppermute(x, "row", [(i, i ^ step) for i in range(row_groups)])

    def array(shape, kind):
        return jax.ShapeDtypeStruct(shape, kind)

    def vs(*xs):
        return [("v", x) for x in xs]

    part_shape = (share, rank)
    places = tile_rows * CODE + tile_cols
    padded = (slots // LANES + 1) * LANES
    codes = jnp.where(jnp.arange(padded) < slots, jnp.pad(places, (0, padded - slots)), counts[0])
    inputs = [("a", codes), ("h", tiles)]
    slot_scratch = [pltpu.SMEM((padded,), jnp.int32), pltpu.VMEM(tiles.shape, BF)]
    sent, kept = call(
        "sketch",
        functools.partial(sketch_kernel, share),
        inputs + [("h", omega)],
        [array((zs * share, rank), BF), array((zs * share, rank), F32)],
        slot_scratch
        + [
            pltpu.VMEM(omega.shape, BF),
            pltpu.VMEM((col_blocks, rows_here, size_b), BF),
            pltpu.SemaphoreType.DMA((LOADS + 2,)),
        ],
        limit=SKETCH_LIMIT,
        flops=2 * rows_here * cols_here * rank,
        nbytes=6 * MIB,
    )
    own, token, *sends = call(
        "pair",
        functools.partial(pair_kernel, share),
        vs(kept, swap_core(sent)),
        [array(part_shape, F32), array(TOKEN, F32)] + [array(part_shape, BF)] * (zs - 1),
        nbytes=MIB,
    )
    gets = [swap_z(x, k + 1) for k, x in enumerate(sends)]
    turned, token = call(
        "turn",
        turn_kernel,
        inputs + [("a", token)],
        [array((RB_DEV, cols_here, size_b), BF), array(TOKEN, F32)],
        slot_scratch + [pltpu.SemaphoreType.DMA((LOADS + 1,))],
        limit=TURN_LIMIT,
        nbytes=8 * MIB,
    )
    own_rows, rows_bf = call(
        "rows",
        functools.partial(rows_kernel, len(gets)),
        vs(own, *gets) + [("a", token)],
        [array(part_shape, F32), array(part_shape, BF)],
        nbytes=MIB,
    )
    chunks = {k: swap_z(rows_bf, k) for k in range(1, zs)}
    order = list(reversed(far_first(zs)))
    (mine,) = call(
        "pack",
        functools.partial(pack_kernel, order),
        vs(rows_bf, *[chunks[k] for k in order]),
        [array((zs * share, rank), BF)],
        nbytes=MIB,
    )
    (full,) = call(
        "full",
        functools.partial(full_kernel, share),
        vs(mine, swap_core(mine)),
        [array((rows_here, rank), BF)],
        nbytes=MIB,
    )
    half = rank // CORES
    gram_shape = (half + half // CORES, half)
    own, gram, *sends = call(
        "back",
        back_kernel,
        vs(turned, full),
        [array((back_share, rank), F32), array(gram_shape, F32)] + [array((back_share, rank), BF)] * (row_groups - 1),
        flops=2 * rows_here * cols_here * rank,
        nbytes=6 * MIB,
    )
    gets = [swap_row(x, k + 1) for k, x in enumerate(sends)]
    (back_sum,) = call(
        "columns",
        functools.partial(columns_kernel, len(gets)),
        vs(own, *gets),
        [array((back_share, rank), BF)],
        nbytes=1,
    )
    backs = [back_sum] + [swap_row(back_sum, k) for k in reversed(range(1, row_groups))]
    terms = [gram] + [swap_row(gram, k) for k in reversed(range(1, row_groups))]
    (gram_sum,) = call("tree", tree_kernel, vs(*terms), [array(gram_shape, F32)], nbytes=1)
    high, low, basis = call(
        "factor",
        functools.partial(factor_kernel, float(total_rows) ** 0.5),
        vs(gram_sum, swap_core(gram_sum), own_rows),
        [array((rank, rank), BF), array((rank, rank), BF), array((share, rank), BF)],
        [pltpu.VMEM((rank, rank), F32), pltpu.VMEM((rank, rank), F32)],
        flops=1,
        nbytes=1,
    )
    (projected,) = call(
        "project",
        functools.partial(project_kernel, float(RB_DEV * row_groups) ** -0.5, row_groups),
        vs(high, low, *backs),
        [array((cols_here, rank), BF)],
        flops=4 * cols_here * rank * rank,
        nbytes=2 * MIB,
    )
    return basis, projected


def solution(mesh):
    return jax.shard_map(
        shards,
        mesh=mesh,
        in_specs=(
            P(("row", "col"), None, None),
            P(("row", "col")),
            P(("row", "col")),
            P(("row", "col")),
            P("col", None),
        ),
        out_specs=(P(("row", "col"), None), P("col", None)),
        check_vma=False,
    )
```

```python
import functools

import jax
import jax.numpy as jnp
from jax import lax
from jax.experimental import pallas as pl
from jax.experimental.pallas import tpu as pltpu
from jax.sharding import PartitionSpec as P

RB_DEV = 16
CORES = 2
SIDES = 2
FACTOR_FLOPS = 40
LOADS = 4
TOKEN = (8, 128)
MIB = 1024 * 1024
BF = jnp.bfloat16
F32 = jnp.float32

NN = (((1,), (0,)), ((), ()))
NT = (((1,), (1,)), ((), ()))
TN = (((0,), (0,)), ((), ()))

SPACES = {"v": pltpu.VMEM, "s": pltpu.SMEM, "h": pltpu.HBM, "a": pl.ANY}


def call(name, body, ins, outs, scratch=(), limit=24, flops=0, nbytes=0):
    return pl.pallas_call(
        body,
        out_shape=outs,
        in_specs=[pl.BlockSpec(memory_space=SPACES[space]) for space, _ in ins],
        out_specs=[pl.BlockSpec(memory_space=pltpu.VMEM) for _ in outs],
        scratch_shapes=list(scratch),
        compiler_params=pltpu.CompilerParams(vmem_limit_bytes=limit * MIB),
        cost_estimate=pl.CostEstimate(flops=flops, bytes_accessed=nbytes, transcendentals=0),
        name=name,
    )(*[pltpu.with_memory_space_constraint(array, pltpu.HBM) if space == "h" else array for space, array in ins])


def dot(a, b, dims=NN):
    return lax.dot_general(a, b, dims, preferred_element_type=F32)


def dot_short(a, b, dims=NN):
    return dot(a.astype(BF), b.astype(BF), dims)


def split(x):
    high = x.astype(BF)
    return high, (x - high.astype(F32)).astype(BF)


def dot_long(a, b, dims=NN):
    a_high, a_low = split(a)
    b_high, b_low = split(b)
    return dot(a_high, b_high, dims) + (dot(a_high, b_low, dims) + dot(a_low, b_high, dims))


def place():
    col = lax.axis_index("col")
    return col // CORES, col % CORES


def far_first(count):
    return [count - 1] + list(range(1, count - 1))


def rows_at(index, count):
    return pl.ds(pl.multiple_of(index * count, count), count)


def put_live(live, places_hbm, places, tiles_hbm, tiles, sems, clear, put):
    load = tiles.shape[0] // LOADS
    rows, cols = places
    firsts = [
        pltpu.make_async_copy(source, target, sems.at[LOADS + k])
        for k, (source, target) in enumerate(zip(places_hbm, places))
    ]
    copies = []
    for k in range(LOADS):
        piece = pl.ds(k * load, load)
        copies.append(pltpu.make_async_copy(tiles_hbm.at[piece], tiles.at[piece], sems.at[k]))
    for copy in firsts + copies:
        copy.start()
    clear()
    for copy in firsts:
        copy.wait()

    def step(slot, carry):
        put(slot, rows[slot], cols[slot])
        return carry

    for k, copy in enumerate(copies):
        copy.wait()
        lax.fori_loop(k * load, jnp.clip(live, k * load, (k + 1) * load), step, 0)


def multiply(share, owner, dense, omega, out):
    for step in range(out.shape[0] // share):
        here = rows_at(step * CORES + owner, share)
        left = jnp.concatenate([dense[c, here, :] for c in range(dense.shape[0])], axis=1)
        out[step * share : (step + 1) * share, :] = dot(left, omega[...]).astype(out.dtype)


def sketch_kernel(share, counts, rows_hbm, cols_hbm, tiles_hbm, omega_hbm, sent, dense, omega, rows, cols, tiles, sems):
    size_b = tiles.shape[1]
    last = pltpu.make_async_copy(omega_hbm, omega, sems.at[LOADS + 2])
    last.start()

    def clear():
        dense[...] = jnp.zeros_like(dense)

    def put(slot, row, col):
        dense[col, rows_at(row, size_b), :] = tiles[slot]

    put_live(counts[0], (rows_hbm, cols_hbm), (rows, cols), tiles_hbm, tiles, sems, clear, put)
    last.wait()
    _, core = place()
    multiply(share, 1 - core, dense, omega, sent)


def kept_kernel(share, dense, omega, kept):
    _, core = place()
    multiply(share, core, dense, omega, kept)


def turn_kernel(counts, rows_hbm, cols_hbm, tiles_hbm, _, turned, token, rows, cols, tiles, sems):
    size_b = tiles.shape[1]
    token[...] = jnp.zeros_like(token)

    def clear():
        turned[...] = jnp.zeros_like(turned)

    def put(slot, row, col):
        turned[row, rows_at(col, size_b), :] = tiles[slot].T

    put_live(counts[0], (rows_hbm, cols_hbm), (rows, cols), tiles_hbm, tiles, sems, clear, put)


def pair_kernel(share, kept, came, own, token, *sends):
    z, _ = place()
    token[...] = jnp.zeros_like(token)
    for step in range(len(sends) + 1):
        here = rows_at(z ^ step, share)
        total = kept[here, :] + came[here, :].astype(F32)
        if step == 0:
            own[...] = total
        else:
            sends[step - 1][...] = total.astype(BF)


def columns_kernel(count, own, *refs):
    total = own[...]
    for ref in refs[:count]:
        total = total + ref[...].astype(F32)
    refs[count][...] = total.astype(BF)


def tree_kernel(count, own, *refs):
    refs[-1][...] = tree_sum([own[...]] + [ref[...] for ref in refs[: count - 1]])


def tree_sum(terms):
    while len(terms) > 1:
        terms = [terms[i] + terms[i + 1] for i in range(0, len(terms), 2)]
    return terms[0]


def rows_kernel(count, own, *refs):
    total = own[...]
    for ref in refs[:count]:
        total = total + ref[...].astype(F32)
    refs[-2][...] = total
    refs[-1][...] = total.astype(BF)


def pack_kernel(order, own, *refs):
    out = refs[-1]
    z, _ = place()
    share = own.shape[0]
    out[rows_at(z, share), :] = own[...]
    for step, ref in zip(order, refs):
        out[rows_at(z ^ step, share), :] = ref[...]


def full_kernel(share, mine, other, full):
    _, core = place()
    for z in range(mine.shape[0] // share):
        here = slice(z * share, (z + 1) * share)
        full[rows_at(z * CORES + core, share), :] = mine[here, :]
        full[rows_at(z * CORES + (1 - core), share), :] = other[here, :]


def gram_kernel(mine, gram):
    z, _ = place()
    half = gram.shape[1]
    quarter = half // SIDES
    for side in range(SIDES):

        @pl.when(z % SIDES == side)
        def _():
            diagonal = mine[:, side * half : (side + 1) * half]
            gram[:half, :] = dot(diagonal, diagonal, TN)
            lower = mine[:, half + side * quarter : half + (side + 1) * quarter]
            gram[half:, :] = dot(lower, mine[:, :half], TN)


def two_kernel(first, second, out):
    out[...] = first[...] + second[...]


def back_kernel(turned, full, _, own, *sends):
    me = lax.axis_index("row")
    share = own.shape[0]
    for step in list(range(1, len(sends) + 1)) + [0]:
        here = rows_at(me ^ step, share)
        left = jnp.concatenate([turned[r, here, :] for r in range(turned.shape[0])], axis=1)
        product = dot(left, full[...])
        if step == 0:
            own[...] = product
        else:
            sends[step - 1][...] = product.astype(BF)


def factor_kernel(scale, *refs):
    mine, other, rows, high, low, basis, work, inverse = refs
    size = work.shape[0]
    half, quarter = size // SIDES, size // (2 * SIDES)
    z, _ = place()
    for side in range(SIDES):
        blocks = jnp.where(z % SIDES == side, mine[...], other[...])
        work[side * half : (side + 1) * half, side * half : (side + 1) * half] = blocks[:half, :]
        work[half + side * quarter : half + (side + 1) * quarter, :half] = blocks[half:, :]
    work[:half, half:] = work[half:, :half].T
    gram = work[...]
    row_id = lax.broadcasted_iota(jnp.int32, (size, size), 0)
    col_id = lax.broadcasted_iota(jnp.int32, (size, size), 1)
    eye = (row_id == col_id).astype(F32)
    diagonal = gram * eye
    scale_col = lax.rsqrt(jnp.sum(diagonal, axis=1, keepdims=True))
    scale_row = lax.rsqrt(jnp.sum(diagonal, axis=0, keepdims=True))
    excess = gram * scale_col * scale_row - eye
    below = (row_id > col_id).astype(F32)
    phi_mask = below + 0.5 * eye
    keep_mask = below + 2.0 * eye
    near = -(excess * phi_mask)
    for step in range(3):
        mul = dot_long if step == 2 else dot_short
        turn = excess + mul(near, excess)
        rest = near * keep_mask + turn + mul(near + turn, near, NT)
        phi = rest * phi_mask
        near = near - phi - mul(phi, near)
    inverse[...] = (near + eye) * scale_row
    converged = jnp.max(jnp.abs(phi)) < 1e-2

    @pl.when(jnp.logical_not(converged))
    def _():
        work[...] = gram * scale_col * scale_row
        inverse[...] = eye

        def eliminate(k, carry):
            row = work[pl.ds(k, 1), :]
            pivot = jnp.sum(jnp.where(col_id[:1] == k, row, 0.0), axis=1, keepdims=True)
            column = jnp.sum(jnp.where(col_id == k, work[...], 0.0), axis=1, keepdims=True)
            factor = jnp.where(row_id[:, :1] > k, column / pivot, 0.0)
            source = inverse[pl.ds(k, 1), :]
            inverse[...] = inverse[...] - factor * source
            inverse[pl.ds(k, 1), :] = source * lax.rsqrt(pivot)
            work[...] = work[...] - factor * row
            return carry

        lax.fori_loop(0, size, eliminate, 0)
        inverse[...] = inverse[...] * scale_row

    high_part, low_part = split(inverse[...] * scale)
    high[...] = high_part
    low[...] = low_part
    row_high, row_low = split(rows[...])
    basis[...] = (
        dot(row_high, high_part, NT) + (dot(row_high, low_part, NT) + dot(row_low, high_part, NT))
    ).astype(BF)


def project_kernel(scale, count, high, low, *refs):
    out = refs[-1]
    me = lax.axis_index("row")
    share = refs[0].shape[0]
    for step in range(count):
        chunk = refs[step][...]
        product = dot(chunk, high[...], NT) + dot(chunk, low[...], NT)
        out[rows_at(me ^ step, share), :] = (product * scale).astype(BF)


def shards(tiles, tile_rows, tile_cols, counts, omega):
    slots, size_b, _ = tiles.shape
    rank = omega.shape[1]
    cols_here = omega.shape[0]
    col_blocks = cols_here // size_b
    row_groups = lax.axis_size("row")
    col_groups = lax.axis_size("col")
    zs = col_groups // CORES
    rows_here = RB_DEV * size_b
    share = rows_here // col_groups
    back_share = cols_here // row_groups
    total_rows = rows_here * row_groups

    def swap_core(x):
        return lax.ppermute(x, "col", [(i, i ^ 1) for i in range(col_groups)])

    def swap_z(x, step):
        return lax.ppermute(x, "col", [(i, i ^ (CORES * step)) for i in range(col_groups)])

    def swap_row(x, step):
        return lax.ppermute(x, "row", [(i, i ^ step) for i in range(row_groups)])

    def array(shape, kind):
        return jax.ShapeDtypeStruct(shape, kind)

    def vs(*xs):
        return [("v", x) for x in xs]

    part_shape = (share, rank)
    inputs = [("s", counts), ("h", tile_rows), ("h", tile_cols), ("h", tiles)]
    slot_scratch = [
        pltpu.SMEM((slots,), jnp.int32),
        pltpu.SMEM((slots,), jnp.int32),
        pltpu.VMEM(tiles.shape, BF),
    ]
    sent, dense, omega_here = call(
        "sketch",
        functools.partial(sketch_kernel, share),
        inputs + [("h", omega)],
        [
            array((zs * share, rank), BF),
            array((col_blocks, rows_here, size_b), BF),
            array(omega.shape, BF),
        ],
        slot_scratch + [pltpu.SemaphoreType.DMA((LOADS + 3,))],
        flops=rows_here * cols_here * rank,
        nbytes=6 * MIB,
    )
    came = swap_core(sent)
    (kept,) = call(
        "kept",
        functools.partial(kept_kernel, share),
        vs(dense, omega_here),
        [array((zs * share, rank), F32)],
        flops=rows_here * cols_here * rank,
        nbytes=1,
    )
    own, token, *sends = call(
        "pair",
        functools.partial(pair_kernel, share),
        vs(kept, came),
        [array(part_shape, F32), array(TOKEN, F32)] + [array(part_shape, BF)] * (zs - 1),
        nbytes=MIB,
    )
    gets = [swap_z(sends[k - 1], k) for k in far_first(zs)]
    turned, token = call(
        "turn",
        turn_kernel,
        inputs + [("a", token)],
        [array((RB_DEV, cols_here, size_b), BF), array(TOKEN, F32)],
        slot_scratch + [pltpu.SemaphoreType.DMA((LOADS + 2,))],
        nbytes=8 * MIB,
    )
    own_rows, rows_bf = call(
        "rows",
        functools.partial(rows_kernel, len(gets)),
        vs(own, *gets) + [("a", token)],
        [array(part_shape, F32), array(part_shape, BF)],
        nbytes=MIB,
    )
    chunks = {k: swap_z(rows_bf, k) for k in range(1, zs)}
    order = far_first(zs)
    (mine,) = call(
        "pack",
        functools.partial(pack_kernel, order),
        vs(rows_bf, *[chunks[k] for k in order]),
        [array((zs * share, rank), BF)],
        nbytes=MIB,
    )
    (full,) = call(
        "full",
        functools.partial(full_kernel, share),
        vs(mine, swap_core(mine)),
        [array((rows_here, rank), BF)],
        nbytes=MIB,
    )
    half = rank // SIDES
    gram_rows = half + half // SIDES
    gram_out = [array((gram_rows, half), F32)]
    (gram,) = call("gram", gram_kernel, vs(mine), gram_out, nbytes=1)
    own, *sends = call(
        "back",
        back_kernel,
        vs(turned, full) + [("a", gram)],
        [array((back_share, rank), F32)] + [array((back_share, rank), BF)] * (row_groups - 1),
        flops=2 * rows_here * cols_here * rank,
        nbytes=6 * MIB,
    )
    gets = [swap_row(x, k + 1) for k, x in enumerate(sends)]
    (back_sum,) = call(
        "columns",
        functools.partial(columns_kernel, len(gets)),
        vs(own, *gets),
        [array((back_share, rank), BF)],
        nbytes=1,
    )
    backs = [back_sum] + [swap_row(back_sum, k) for k in range(1, row_groups)]
    terms = [gram] + [swap_row(gram, k) for k in range(1, row_groups)]
    (gram,) = call("tree", functools.partial(tree_kernel, len(terms)), vs(*terms) + [("a", own)], gram_out, nbytes=1)
    (gram,) = call("two", two_kernel, vs(gram, swap_core(gram)), gram_out, nbytes=1)
    high, low, basis = call(
        "factor",
        functools.partial(factor_kernel, float(total_rows) ** 0.5),
        vs(gram, swap_z(gram, 1), own_rows),
        [array((rank, rank), BF), array((rank, rank), BF), array((share, rank), BF)],
        [pltpu.VMEM((rank, rank), F32), pltpu.VMEM((rank, rank), F32)],
        flops=int(FACTOR_FLOPS * rank**3),
        nbytes=1,
    )
    (projected,) = call(
        "project",
        functools.partial(project_kernel, float(RB_DEV * row_groups) ** -0.5, row_groups),
        vs(high, low, *backs),
        [array((cols_here, rank), BF)],
        flops=4 * cols_here * rank * rank,
        nbytes=2 * MIB,
    )
    return basis, projected


def solution(mesh):
    return jax.shard_map(
        shards,
        mesh=mesh,
        in_specs=(
            P(("row", "col"), None, None),
            P(("row", "col")),
            P(("row", "col")),
            P(("row", "col")),
            P("col", None),
        ),
        out_specs=(P(("row", "col"), None), P("col", None)),
        check_vma=False,
    )
```

```python
import functools

import jax
import jax.numpy as jnp
from jax import lax
from jax.experimental import pallas as pl
from jax.experimental.pallas import tpu as pltpu
from jax.sharding import PartitionSpec as P

RB_DEV = 16
CORES = 2
SIDES = 2
FACTOR_FLOPS = 45
LOADS = 8
TOKEN = (8, 128)
MIB = 1024 * 1024
BF = jnp.bfloat16
F32 = jnp.float32

NN = (((1,), (0,)), ((), ()))
NT = (((1,), (1,)), ((), ()))
TN = (((0,), (0,)), ((), ()))

SPACES = {"v": pltpu.VMEM, "s": pltpu.SMEM, "h": pltpu.HBM, "a": pl.ANY}


def call(name, body, ins, outs, scratch=(), limit=24, flops=0, nbytes=0):
    return pl.pallas_call(
        body,
        out_shape=outs,
        in_specs=[pl.BlockSpec(memory_space=SPACES[space]) for space, _ in ins],
        out_specs=[pl.BlockSpec(memory_space=pltpu.VMEM) for _ in outs],
        scratch_shapes=list(scratch),
        compiler_params=pltpu.CompilerParams(vmem_limit_bytes=limit * MIB),
        cost_estimate=pl.CostEstimate(flops=flops, bytes_accessed=nbytes, transcendentals=0),
        name=name,
    )(*[pltpu.with_memory_space_constraint(array, pltpu.HBM) if space == "h" else array for space, array in ins])


def dot(a, b, dims=NN):
    return lax.dot_general(a, b, dims, preferred_element_type=F32)


def dot_short(a, b, dims=NN):
    return dot(a.astype(BF), b.astype(BF), dims)


def split(x):
    high = x.astype(BF)
    return high, (x - high.astype(F32)).astype(BF)


def dot_long(a, b, dims=NN):
    a_high, a_low = split(a)
    b_high, b_low = split(b)
    return dot(a_high, b_high, dims) + (dot(a_high, b_low, dims) + dot(a_low, b_high, dims))


def place():
    col = lax.axis_index("col")
    return col // CORES, col % CORES


def far_first(count):
    return [count - 1] + list(range(1, count - 1))


def rows_at(index, count):
    return pl.ds(pl.multiple_of(index * count, count), count)


def put_live(live, places_hbm, places, tiles_hbm, tiles, sems, clear, put):
    load = tiles.shape[0] // LOADS
    rows, cols = places
    firsts = [
        pltpu.make_async_copy(source, target, sems.at[LOADS + k])
        for k, (source, target) in enumerate(zip(places_hbm, places))
    ]
    for copy in firsts:
        copy.start()

    def bring(k):
        piece = pl.ds(k * load, load)
        return pltpu.make_async_copy(tiles_hbm.at[piece], tiles.at[piece], sems.at[k])

    for k in range(LOADS):

        @pl.when(live > k * load)
        def _():
            bring(k).start()

    clear()
    for copy in firsts:
        copy.wait()

    def step(slot, carry):
        put(slot, rows[slot], cols[slot])
        return carry

    for k in range(LOADS):

        @pl.when(live > k * load)
        def _():
            bring(k).wait()
            lax.fori_loop(k * load, jnp.minimum(live, (k + 1) * load), step, 0)


def multiply(share, owner, dense, omega, out):
    for step in range(out.shape[0] // share):
        here = rows_at(step * CORES + owner, share)
        left = jnp.concatenate([dense[c, here, :] for c in range(dense.shape[0])], axis=1)
        out[step * share : (step + 1) * share, :] = dot(left, omega[...]).astype(out.dtype)


def sketch_kernel(share, counts, rows_hbm, cols_hbm, tiles_hbm, omega_hbm, sent, dense, omega, rows, cols, tiles, sems):
    size_b = tiles.shape[1]
    last = pltpu.make_async_copy(omega_hbm, omega, sems.at[LOADS + 2])
    last.start()

    def clear():
        dense[...] = jnp.zeros_like(dense)

    def put(slot, row, col):
        dense[col, rows_at(row, size_b), :] = tiles[slot]

    put_live(counts[0], (rows_hbm, cols_hbm), (rows, cols), tiles_hbm, tiles, sems, clear, put)
    last.wait()
    _, core = place()
    multiply(share, 1 - core, dense, omega, sent)


def kept_kernel(share, dense, omega, kept):
    _, core = place()
    multiply(share, core, dense, omega, kept)


def turn_kernel(counts, rows_hbm, cols_hbm, tiles_hbm, _, turned, token, rows, cols, tiles, sems):
    size_b = tiles.shape[1]
    token[...] = jnp.zeros_like(token)

    def clear():
        turned[...] = jnp.zeros_like(turned)

    def put(slot, row, col):
        turned[row, rows_at(col, size_b), :] = tiles[slot].T

    put_live(counts[0], (rows_hbm, cols_hbm), (rows, cols), tiles_hbm, tiles, sems, clear, put)


def pair_kernel(share, kept, came, own, token, *sends):
    z, _ = place()
    token[...] = jnp.zeros_like(token)
    for step in range(len(sends) + 1):
        here = rows_at(z ^ step, share)
        total = kept[here, :] + came[here, :].astype(F32)
        if step == 0:
            own[...] = total
        else:
            sends[step - 1][...] = total.astype(BF)


def columns_kernel(count, own, *refs):
    total = own[...]
    for ref in refs[:count]:
        total = total + ref[...].astype(F32)
    refs[count][...] = total.astype(BF)


def tree_kernel(count, own, *refs):
    refs[-1][...] = tree_sum([own[...]] + [ref[...] for ref in refs[: count - 1]])


def tree_sum(terms):
    while len(terms) > 1:
        terms = [terms[i] + terms[i + 1] for i in range(0, len(terms), 2)]
    return terms[0]


def rows_kernel(count, own, *refs):
    total = own[...]
    for ref in refs[:count]:
        total = total + ref[...].astype(F32)
    refs[-2][...] = total
    refs[-1][...] = total.astype(BF)


def pack_kernel(order, own, *refs):
    out = refs[-1]
    z, _ = place()
    share = own.shape[0]
    out[rows_at(z, share), :] = own[...]
    for step, ref in zip(order, refs):
        out[rows_at(z ^ step, share), :] = ref[...]


def full_kernel(share, mine, other, full):
    _, core = place()
    for z in range(mine.shape[0] // share):
        here = slice(z * share, (z + 1) * share)
        full[rows_at(z * CORES + core, share), :] = mine[here, :]
        full[rows_at(z * CORES + (1 - core), share), :] = other[here, :]


def gram_kernel(mine, gram):
    z, _ = place()
    half = gram.shape[1]
    quarter, eighth = half // 2, half // 4
    for side in range(SIDES):

        @pl.when(z % SIDES == side)
        def _():
            columns = mine[:, side * half : (side + 1) * half]
            block = dot(columns, columns, TN)
            lower = mine[:, half + side * quarter : half + (side + 1) * quarter]
            gram[:quarter, :quarter] = block[:quarter, :quarter]
            gram[:quarter, quarter:] = block[quarter:, quarter:]
            gram[quarter : quarter + eighth, :quarter] = block[quarter : quarter + eighth, :quarter]
            gram[quarter : quarter + eighth, quarter:] = block[quarter + eighth :, :quarter]
            gram[quarter + eighth :, :] = dot(lower, mine[:, :half], TN)


def unpack(blocks, side, work):
    half = blocks.shape[1]
    quarter, eighth = half // 2, half // 4
    first = side * half
    middle, last = first + quarter, first + half
    work[first:middle, first:middle] = blocks[:quarter, :quarter]
    work[middle:last, middle:last] = blocks[:quarter, quarter:]
    below = jnp.concatenate(
        [blocks[quarter : quarter + eighth, :quarter], blocks[quarter : quarter + eighth, quarter:]], axis=0
    )
    work[middle:last, first:middle] = below
    work[first:middle, middle:last] = below.T
    work[half + side * quarter : half + (side + 1) * quarter, :half] = blocks[quarter + eighth :, :]


def two_kernel(first, second, out):
    out[...] = first[...] + second[...]


def back_kernel(turned, full, _, own, *sends):
    me = lax.axis_index("row")
    share = own.shape[0]
    for step in list(range(1, len(sends) + 1)) + [0]:
        here = rows_at(me ^ step, share)
        left = jnp.concatenate([turned[r, here, :] for r in range(turned.shape[0])], axis=1)
        product = dot(left, full[...])
        if step == 0:
            own[...] = product
        else:
            sends[step - 1][...] = product.astype(BF)


def factor_kernel(scale, *refs):
    mine, other, rows, high, low, basis, work, inverse = refs
    size = work.shape[0]
    half = size // SIDES
    z, _ = place()
    for side in range(SIDES):
        unpack(jnp.where(z % SIDES == side, mine[...], other[...]), side, work)
    work[:half, half:] = work[half:, :half].T
    gram = work[...]
    row_id = lax.broadcasted_iota(jnp.int32, (size, size), 0)
    col_id = lax.broadcasted_iota(jnp.int32, (size, size), 1)
    eye = (row_id == col_id).astype(F32)
    diagonal = gram * eye
    scale_col = lax.rsqrt(jnp.sum(diagonal, axis=1, keepdims=True))
    scale_row = lax.rsqrt(jnp.sum(diagonal, axis=0, keepdims=True))
    excess = gram * scale_col * scale_row - eye
    below = (row_id > col_id).astype(F32)
    phi_mask = below + 0.5 * eye
    keep_mask = below + 2.0 * eye
    near = -(excess * phi_mask)
    for step in range(3):
        mul = dot_long if step == 2 else dot_short
        turn = excess + mul(near, excess)
        rest = near * keep_mask + turn + mul(near + turn, near, NT)
        phi = rest * phi_mask
        near = near - phi - mul(phi, near)
    inverse[...] = (near + eye) * scale_row
    converged = jnp.sum(phi * phi) < 4e-4

    @pl.when(jnp.logical_not(converged))
    def _():
        work[...] = gram * scale_col * scale_row
        inverse[...] = eye

        def eliminate(k, carry):
            row = work[pl.ds(k, 1), :]
            pivot = jnp.sum(jnp.where(col_id[:1] == k, row, 0.0), axis=1, keepdims=True)
            column = jnp.sum(jnp.where(col_id == k, work[...], 0.0), axis=1, keepdims=True)
            factor = jnp.where(row_id[:, :1] > k, column / pivot, 0.0)
            source = inverse[pl.ds(k, 1), :]
            inverse[...] = inverse[...] - factor * source
            inverse[pl.ds(k, 1), :] = source * lax.rsqrt(pivot)
            work[...] = work[...] - factor * row
            return carry

        lax.fori_loop(0, size, eliminate, 0)
        inverse[...] = inverse[...] * scale_row

    high_part, low_part = split(inverse[...] * scale)
    high[...] = high_part
    low[...] = low_part
    row_high, row_low = split(rows[...])
    basis[...] = (
        dot(row_high, high_part, NT) + (dot(row_high, low_part, NT) + dot(row_low, high_part, NT))
    ).astype(BF)


def project_kernel(scale, count, high, low, *refs):
    out = refs[-1]
    me = lax.axis_index("row")
    share = refs[0].shape[0]
    for step in range(count):
        chunk = refs[step][...]
        product = dot(chunk, high[...], NT) + dot(chunk, low[...], NT)
        out[rows_at(me ^ step, share), :] = (product * scale).astype(BF)


def shards(tiles, tile_rows, tile_cols, counts, omega):
    slots, size_b, _ = tiles.shape
    rank = omega.shape[1]
    cols_here = omega.shape[0]
    col_blocks = cols_here // size_b
    row_groups = lax.axis_size("row")
    col_groups = lax.axis_size("col")
    zs = col_groups // CORES
    rows_here = RB_DEV * size_b
    share = rows_here // col_groups
    back_share = cols_here // row_groups
    total_rows = rows_here * row_groups

    def swap_core(x):
        return lax.ppermute(x, "col", [(i, i ^ 1) for i in range(col_groups)])

    def swap_z(x, step):
        return lax.ppermute(x, "col", [(i, i ^ (CORES * step)) for i in range(col_groups)])

    def swap_row(x, step):
        return lax.ppermute(x, "row", [(i, i ^ step) for i in range(row_groups)])

    def array(shape, kind):
        return jax.ShapeDtypeStruct(shape, kind)

    def vs(*xs):
        return [("v", x) for x in xs]

    part_shape = (share, rank)
    inputs = [("s", counts), ("h", tile_rows), ("h", tile_cols), ("h", tiles)]
    slot_scratch = [
        pltpu.SMEM((slots,), jnp.int32),
        pltpu.SMEM((slots,), jnp.int32),
        pltpu.VMEM(tiles.shape, BF),
    ]
    sent, dense, omega_here = call(
        "sketch",
        functools.partial(sketch_kernel, share),
        inputs + [("h", omega)],
        [
            array((zs * share, rank), BF),
            array((col_blocks, rows_here, size_b), BF),
            array(omega.shape, BF),
        ],
        slot_scratch + [pltpu.SemaphoreType.DMA((LOADS + 3,))],
        flops=rows_here * cols_here * rank,
        nbytes=6 * MIB,
    )
    came = swap_core(sent)
    (kept,) = call(
        "kept",
        functools.partial(kept_kernel, share),
        vs(dense, omega_here),
        [array((zs * share, rank), F32)],
        flops=rows_here * cols_here * rank,
        nbytes=1,
    )
    own, token, *sends = call(
        "pair",
        functools.partial(pair_kernel, share),
        vs(kept, came),
        [array(part_shape, F32), array(TOKEN, F32)] + [array(part_shape, BF)] * (zs - 1),
        nbytes=MIB,
    )
    gets = [swap_z(sends[k - 1], k) for k in far_first(zs)]
    turned, token = call(
        "turn",
        turn_kernel,
        inputs + [("a", token)],
        [array((RB_DEV, cols_here, size_b), BF), array(TOKEN, F32)],
        slot_scratch + [pltpu.SemaphoreType.DMA((LOADS + 2,))],
        nbytes=8 * MIB,
    )
    own_rows, rows_bf = call(
        "rows",
        functools.partial(rows_kernel, len(gets)),
        vs(own, *gets) + [("a", token)],
        [array(part_shape, F32), array(part_shape, BF)],
        nbytes=MIB,
    )
    chunks = {k: swap_z(rows_bf, k) for k in range(1, zs)}
    order = far_first(zs)
    (mine,) = call(
        "pack",
        functools.partial(pack_kernel, order),
        vs(rows_bf, *[chunks[k] for k in order]),
        [array((zs * share, rank), BF)],
        nbytes=MIB,
    )
    (full,) = call(
        "full",
        functools.partial(full_kernel, share),
        vs(mine, swap_core(mine)),
        [array((rows_here, rank), BF)],
        nbytes=MIB,
    )
    half = rank // SIDES
    gram_rows = half // 2 + half // 4 + half // 2
    gram_out = [array((gram_rows, half), F32)]
    (gram,) = call("gram", gram_kernel, vs(mine), gram_out, nbytes=1)
    own, *sends = call(
        "back",
        back_kernel,
        vs(turned, full) + [("a", gram)],
        [array((back_share, rank), F32)] + [array((back_share, rank), BF)] * (row_groups - 1),
        flops=2 * rows_here * cols_here * rank,
        nbytes=6 * MIB,
    )
    gets = [swap_row(x, k + 1) for k, x in enumerate(sends)]
    (back_sum,) = call(
        "columns",
        functools.partial(columns_kernel, len(gets)),
        vs(own, *gets),
        [array((back_share, rank), BF)],
        nbytes=1,
    )
    backs = [back_sum] + [swap_row(back_sum, k) for k in range(1, row_groups)]
    terms = [gram] + [swap_row(gram, k) for k in range(1, row_groups)]
    (gram,) = call("tree", functools.partial(tree_kernel, len(terms)), vs(*terms) + [("a", own)], gram_out, nbytes=1)
    (gram,) = call("two", two_kernel, vs(gram, swap_core(gram)), gram_out, nbytes=1)
    high, low, basis = call(
        "factor",
        functools.partial(factor_kernel, float(total_rows) ** 0.5),
        vs(gram, swap_z(gram, 1), own_rows),
        [array((rank, rank), BF), array((rank, rank), BF), array((share, rank), BF)],
        [pltpu.VMEM((rank, rank), F32), pltpu.VMEM((rank, rank), F32)],
        flops=int(FACTOR_FLOPS * rank**3),
        nbytes=1,
    )
    (projected,) = call(
        "project",
        functools.partial(project_kernel, float(RB_DEV * row_groups) ** -0.5, row_groups),
        vs(high, low, *backs),
        [array((cols_here, rank), BF)],
        flops=4 * cols_here * rank * rank,
        nbytes=2 * MIB,
    )
    return basis, projected


def solution(mesh):
    return jax.shard_map(
        shards,
        mesh=mesh,
        in_specs=(
            P(("row", "col"), None, None),
            P(("row", "col")),
            P(("row", "col")),
            P(("row", "col")),
            P("col", None),
        ),
        out_specs=(P(("row", "col"), None), P("col", None)),
        check_vma=False,
    )
```

```python
import functools

import jax
import jax.numpy as jnp
from jax import lax
from jax.experimental import pallas as pl
from jax.experimental.pallas import tpu as pltpu
from jax.sharding import PartitionSpec as P

RB_DEV = 16
CORES = 2
SIDES = 2
FACTOR_FLOPS = 45
LOADS = 8
TOKEN = (8, 128)
MIB = 1024 * 1024
BF = jnp.bfloat16
F32 = jnp.float32

NN = (((1,), (0,)), ((), ()))
NT = (((1,), (1,)), ((), ()))
TN = (((0,), (0,)), ((), ()))

SPACES = {"v": pltpu.VMEM, "s": pltpu.SMEM, "h": pltpu.HBM, "a": pl.ANY}


def call(name, body, ins, outs, scratch=(), limit=24, flops=0, nbytes=0):
    return pl.pallas_call(
        body,
        out_shape=outs,
        in_specs=[pl.BlockSpec(memory_space=SPACES[space]) for space, _ in ins],
        out_specs=[pl.BlockSpec(memory_space=pltpu.VMEM) for _ in outs],
        scratch_shapes=list(scratch),
        compiler_params=pltpu.CompilerParams(vmem_limit_bytes=limit * MIB),
        cost_estimate=pl.CostEstimate(flops=flops, bytes_accessed=nbytes, transcendentals=0),
        name=name,
    )(*[pltpu.with_memory_space_constraint(array, pltpu.HBM) if space == "h" else array for space, array in ins])


def dot(a, b, dims=NN):
    return lax.dot_general(a, b, dims, preferred_element_type=F32)


def dot_short(a, b, dims=NN):
    return dot(a.astype(BF), b.astype(BF), dims)


def split(x):
    high = x.astype(BF)
    return high, (x - high.astype(F32)).astype(BF)


def dot_long(a, b, dims=NN):
    a_high, a_low = split(a)
    b_high, b_low = split(b)
    return dot(a_high, b_high, dims) + (dot(a_high, b_low, dims) + dot(a_low, b_high, dims))


def place():
    col = lax.axis_index("col")
    return col // CORES, col % CORES


def far_first(count):
    return [count - 1] + list(range(1, count - 1))


def rows_at(index, count):
    return pl.ds(pl.multiple_of(index * count, count), count)


def put_live(live, places_hbm, places, tiles_hbm, tiles, sems, clear, put):
    load = tiles.shape[0] // LOADS
    rows, cols = places
    firsts = [
        pltpu.make_async_copy(source, target, sems.at[LOADS + k])
        for k, (source, target) in enumerate(zip(places_hbm, places))
    ]
    for copy in firsts:
        copy.start()

    def bring(k):
        piece = pl.ds(k * load, load)
        return pltpu.make_async_copy(tiles_hbm.at[piece], tiles.at[piece], sems.at[k])

    for k in range(LOADS):

        @pl.when(live > k * load)
        def _():
            bring(k).start()

    clear()
    for copy in firsts:
        copy.wait()

    def step(slot, carry):
        put(slot, rows[slot], cols[slot])
        return carry

    for k in range(LOADS):

        @pl.when(live > k * load)
        def _():
            bring(k).wait()
            lax.fori_loop(k * load, jnp.minimum(live, (k + 1) * load), step, 0)


def multiply(share, owner, dense, omega, out):
    for step in range(out.shape[0] // share):
        here = rows_at(step * CORES + owner, share)
        left = jnp.concatenate([dense[c, here, :] for c in range(dense.shape[0])], axis=1)
        out[step * share : (step + 1) * share, :] = dot(left, omega[...]).astype(out.dtype)


def sketch_kernel(share, counts, rows_hbm, cols_hbm, tiles_hbm, omega_hbm, sent, dense, omega, rows, cols, tiles, sems):
    size_b = tiles.shape[1]
    last = pltpu.make_async_copy(omega_hbm, omega, sems.at[LOADS + 2])

    def clear():
        last.start()
        dense[...] = jnp.zeros_like(dense)

    def put(slot, row, col):
        dense[col, rows_at(row, size_b), :] = tiles[slot]

    put_live(counts[0], (rows_hbm, cols_hbm), (rows, cols), tiles_hbm, tiles, sems, clear, put)
    last.wait()
    _, core = place()
    multiply(share, 1 - core, dense, omega, sent)


def kept_kernel(share, dense, omega, kept):
    _, core = place()
    multiply(share, core, dense, omega, kept)


def turn_kernel(counts, rows_hbm, cols_hbm, tiles_hbm, _, turned, token, rows, cols, tiles, sems):
    size_b = tiles.shape[1]
    token[...] = jnp.zeros_like(token)

    def clear():
        turned[...] = jnp.zeros_like(turned)

    def put(slot, row, col):
        turned[row, rows_at(col, size_b), :] = tiles[slot].T

    put_live(counts[0], (rows_hbm, cols_hbm), (rows, cols), tiles_hbm, tiles, sems, clear, put)


def pair_kernel(share, kept, came, own, token, *sends):
    z, _ = place()
    token[...] = jnp.zeros_like(token)
    for step in range(len(sends) + 1):
        here = rows_at(z ^ step, share)
        total = kept[here, :] + came[here, :].astype(F32)
        if step == 0:
            own[...] = total
        else:
            sends[step - 1][...] = total.astype(BF)


def columns_kernel(count, own, *refs):
    total = own[...]
    for ref in refs[:count]:
        total = total + ref[...].astype(F32)
    refs[count][...] = total.astype(BF)


def tree_kernel(count, own, *refs):
    refs[-1][...] = tree_sum([own[...]] + [ref[...] for ref in refs[: count - 1]])


def tree_sum(terms):
    while len(terms) > 1:
        terms = [terms[i] + terms[i + 1] for i in range(0, len(terms), 2)]
    return terms[0]


def rows_kernel(count, own, *refs):
    total = own[...]
    for ref in refs[:count]:
        total = total + ref[...].astype(F32)
    refs[-2][...] = total
    refs[-1][...] = total.astype(BF)


def pack_kernel(order, own, *refs):
    out = refs[-1]
    z, _ = place()
    share = own.shape[0]
    out[rows_at(z, share), :] = own[...]
    for step, ref in zip(order, refs):
        out[rows_at(z ^ step, share), :] = ref[...]


def full_kernel(share, mine, other, full):
    _, core = place()
    for z in range(mine.shape[0] // share):
        here = slice(z * share, (z + 1) * share)
        full[rows_at(z * CORES + core, share), :] = mine[here, :]
        full[rows_at(z * CORES + (1 - core), share), :] = other[here, :]


def gram_kernel(mine, gram):
    z, _ = place()
    half = gram.shape[1]
    quarter, eighth = half // 2, half // 4
    for side in range(SIDES):

        @pl.when(z % SIDES == side)
        def _():
            columns = mine[:, side * half : (side + 1) * half]
            block = dot(columns, columns, TN)
            lower = mine[:, half + side * quarter : half + (side + 1) * quarter]
            gram[:quarter, :quarter] = block[:quarter, :quarter]
            gram[:quarter, quarter:] = block[quarter:, quarter:]
            gram[quarter : quarter + eighth, :quarter] = block[quarter : quarter + eighth, :quarter]
            gram[quarter : quarter + eighth, quarter:] = block[quarter + eighth :, :quarter]
            gram[quarter + eighth :, :] = dot(lower, mine[:, :half], TN)


def unpack(blocks, side, work):
    half = blocks.shape[1]
    quarter, eighth = half // 2, half // 4
    first = side * half
    middle, last = first + quarter, first + half
    work[first:middle, first:middle] = blocks[:quarter, :quarter]
    work[middle:last, middle:last] = blocks[:quarter, quarter:]
    below = jnp.concatenate(
        [blocks[quarter : quarter + eighth, :quarter], blocks[quarter : quarter + eighth, quarter:]], axis=0
    )
    work[middle:last, first:middle] = below
    work[first:middle, middle:last] = below.T
    work[half + side * quarter : half + (side + 1) * quarter, :half] = blocks[quarter + eighth :, :]


def two_kernel(first, second, out):
    out[...] = first[...] + second[...]


def back_kernel(turned, full, _, own, *sends):
    me = lax.axis_index("row")
    share = own.shape[0]
    for step in list(range(1, len(sends) + 1)) + [0]:
        here = rows_at(me ^ step, share)
        left = jnp.concatenate([turned[r, here, :] for r in range(turned.shape[0])], axis=1)
        product = dot(left, full[...])
        if step == 0:
            own[...] = product
        else:
            sends[step - 1][...] = product.astype(BF)


def factor_kernel(scale, *refs):
    mine, other, rows, high, low, basis, work, inverse = refs
    size = work.shape[0]
    half = size // SIDES
    z, _ = place()
    for side in range(SIDES):
        unpack(jnp.where(z % SIDES == side, mine[...], other[...]), side, work)
    work[:half, half:] = work[half:, :half].T
    gram = work[...]
    row_id = lax.broadcasted_iota(jnp.int32, (size, size), 0)
    col_id = lax.broadcasted_iota(jnp.int32, (size, size), 1)
    eye = (row_id == col_id).astype(F32)
    diagonal = gram * eye
    scale_col = lax.rsqrt(jnp.sum(diagonal, axis=1, keepdims=True))
    scale_row = lax.rsqrt(jnp.sum(diagonal, axis=0, keepdims=True))
    excess = gram * scale_col * scale_row - eye
    below = (row_id > col_id).astype(F32)
    phi_mask = below + 0.5 * eye
    keep_mask = below + 2.0 * eye
    near = -(excess * phi_mask)
    for step in range(3):
        mul = dot_long if step == 2 else dot_short
        turn = excess + mul(near, excess)
        rest = near * keep_mask + turn + mul(near + turn, near, NT)
        phi = rest * phi_mask
        near = near - phi - mul(phi, near)
    inverse[...] = (near + eye) * scale_row
    converged = jnp.sum(phi * phi) < 4e-4

    @pl.when(jnp.logical_not(converged))
    def _():
        work[...] = gram * scale_col * scale_row
        inverse[...] = eye

        def eliminate(k, carry):
            row = work[pl.ds(k, 1), :]
            pivot = jnp.sum(jnp.where(col_id[:1] == k, row, 0.0), axis=1, keepdims=True)
            column = jnp.sum(jnp.where(col_id == k, work[...], 0.0), axis=1, keepdims=True)
            factor = jnp.where(row_id[:, :1] > k, column / pivot, 0.0)
            source = inverse[pl.ds(k, 1), :]
            inverse[...] = inverse[...] - factor * source
            inverse[pl.ds(k, 1), :] = source * lax.rsqrt(pivot)
            work[...] = work[...] - factor * row
            return carry

        lax.fori_loop(0, size, eliminate, 0)
        inverse[...] = inverse[...] * scale_row

    high_part, low_part = split(inverse[...] * scale)
    high[...] = high_part
    low[...] = low_part
    row_high, row_low = split(rows[...])
    basis[...] = (
        dot(row_high, high_part, NT) + (dot(row_high, low_part, NT) + dot(row_low, high_part, NT))
    ).astype(BF)


def project_kernel(scale, count, high, low, *refs):
    out, work, sems = refs[-3:]
    me = lax.axis_index("row")
    share = refs[0].shape[0]
    copies = []
    for step in range(count):
        chunk = refs[step][...]
        product = dot(chunk, high[...], NT) + dot(chunk, low[...], NT)
        work[step * share : (step + 1) * share, :] = (product * scale).astype(BF)
        copies.append(
            pltpu.make_async_copy(
                work.at[pl.ds(step * share, share)], out.at[rows_at(me ^ step, share)], sems.at[step]
            )
        )
        copies[-1].start()
    for copy in copies:
        copy.wait()


def shards(tiles, tile_rows, tile_cols, counts, omega):
    slots, size_b, _ = tiles.shape
    rank = omega.shape[1]
    cols_here = omega.shape[0]
    col_blocks = cols_here // size_b
    row_groups = lax.axis_size("row")
    col_groups = lax.axis_size("col")
    zs = col_groups // CORES
    rows_here = RB_DEV * size_b
    share = rows_here // col_groups
    back_share = cols_here // row_groups
    total_rows = rows_here * row_groups

    def swap_core(x):
        return lax.ppermute(x, "col", [(i, i ^ 1) for i in range(col_groups)])

    def swap_z(x, step):
        return lax.ppermute(x, "col", [(i, i ^ (CORES * step)) for i in range(col_groups)])

    def swap_row(x, step):
        return lax.ppermute(x, "row", [(i, i ^ step) for i in range(row_groups)])

    def array(shape, kind):
        return jax.ShapeDtypeStruct(shape, kind)

    def vs(*xs):
        return [("v", x) for x in xs]

    part_shape = (share, rank)
    inputs = [("s", counts), ("h", tile_rows), ("h", tile_cols), ("h", tiles)]
    slot_scratch = [
        pltpu.SMEM((slots,), jnp.int32),
        pltpu.SMEM((slots,), jnp.int32),
        pltpu.VMEM(tiles.shape, BF),
    ]
    sent, dense, omega_here = call(
        "sketch",
        functools.partial(sketch_kernel, share),
        inputs + [("h", omega)],
        [
            array((zs * share, rank), BF),
            array((col_blocks, rows_here, size_b), BF),
            array(omega.shape, BF),
        ],
        slot_scratch + [pltpu.SemaphoreType.DMA((LOADS + 3,))],
        flops=rows_here * cols_here * rank,
        nbytes=6 * MIB,
    )
    came = swap_core(sent)
    (kept,) = call(
        "kept",
        functools.partial(kept_kernel, share),
        vs(dense, omega_here),
        [array((zs * share, rank), F32)],
        flops=rows_here * cols_here * rank,
        nbytes=1,
    )
    own, token, *sends = call(
        "pair",
        functools.partial(pair_kernel, share),
        vs(kept, came),
        [array(part_shape, F32), array(TOKEN, F32)] + [array(part_shape, BF)] * (zs - 1),
        nbytes=MIB,
    )
    gets = [swap_z(sends[k - 1], k) for k in far_first(zs)]
    turned, token = call(
        "turn",
        turn_kernel,
        inputs + [("a", token)],
        [array((RB_DEV, cols_here, size_b), BF), array(TOKEN, F32)],
        slot_scratch + [pltpu.SemaphoreType.DMA((LOADS + 2,))],
        nbytes=8 * MIB,
    )
    own_rows, rows_bf = call(
        "rows",
        functools.partial(rows_kernel, len(gets)),
        vs(own, *gets) + [("a", token)],
        [array(part_shape, F32), array(part_shape, BF)],
        nbytes=MIB,
    )
    chunks = {k: swap_z(rows_bf, k) for k in range(1, zs)}
    order = far_first(zs)
    (mine,) = call(
        "pack",
        functools.partial(pack_kernel, order),
        vs(rows_bf, *[chunks[k] for k in order]),
        [array((zs * share, rank), BF)],
        nbytes=MIB,
    )
    (full,) = call(
        "full",
        functools.partial(full_kernel, share),
        vs(mine, swap_core(mine)),
        [array((rows_here, rank), BF)],
        nbytes=MIB,
    )
    half = rank // SIDES
    gram_rows = half // 2 + half // 4 + half // 2
    gram_out = [array((gram_rows, half), F32)]
    (gram,) = call("gram", gram_kernel, vs(mine), gram_out, nbytes=1)
    own, *sends = call(
        "back",
        back_kernel,
        vs(turned, full) + [("a", gram)],
        [array((back_share, rank), F32)] + [array((back_share, rank), BF)] * (row_groups - 1),
        flops=2 * rows_here * cols_here * rank,
        nbytes=6 * MIB,
    )
    gets = [swap_row(x, k + 1) for k, x in enumerate(sends)]
    (back_sum,) = call(
        "columns",
        functools.partial(columns_kernel, len(gets)),
        vs(own, *gets),
        [array((back_share, rank), BF)],
        nbytes=1,
    )
    backs = [back_sum] + [swap_row(back_sum, k) for k in range(1, row_groups)]
    terms = [gram] + [swap_row(gram, k) for k in range(1, row_groups)]
    (gram,) = call("tree", functools.partial(tree_kernel, len(terms)), vs(*terms) + [("a", own)], gram_out, nbytes=1)
    (gram,) = call("two", two_kernel, vs(gram, swap_core(gram)), gram_out, nbytes=1)
    high, low, basis = call(
        "factor",
        functools.partial(factor_kernel, float(total_rows) ** 0.5),
        vs(gram, swap_z(gram, 1), own_rows),
        [array((rank, rank), BF), array((rank, rank), BF), array((share, rank), BF)],
        [pltpu.VMEM((rank, rank), F32), pltpu.VMEM((rank, rank), F32)],
        flops=int(FACTOR_FLOPS * rank**3),
        nbytes=1,
    )
    ins = [high, low, *backs]
    projected = pl.pallas_call(
        functools.partial(project_kernel, float(RB_DEV * row_groups) ** -0.5, row_groups),
        out_shape=pltpu.HBM((cols_here, rank), BF),
        in_specs=[pl.BlockSpec(memory_space=pltpu.VMEM)] * len(ins),
        out_specs=pl.BlockSpec(memory_space=pltpu.HBM),
        scratch_shapes=[pltpu.VMEM((cols_here, rank), BF), pltpu.SemaphoreType.DMA((row_groups,))],
        compiler_params=pltpu.CompilerParams(vmem_limit_bytes=24 * MIB),
        cost_estimate=pl.CostEstimate(flops=4 * cols_here * rank * rank, bytes_accessed=2 * MIB, transcendentals=0),
        name="project",
    )(*ins)
    return basis, projected


def solution(mesh):
    return jax.shard_map(
        shards,
        mesh=mesh,
        in_specs=(
            P(("row", "col"), None, None),
            P(("row", "col")),
            P(("row", "col")),
            P(("row", "col")),
            P("col", None),
        ),
        out_specs=(P(("row", "col"), None), P("col", None)),
        check_vma=False,
    )
```
